32 devices in a mesh: gx: 16 (over z, y, x), gy: 2 (over core).
Axes of the slice: x: 2, y: 2, z: 4, core: 2. Of those that a mesh axis runs over, the one named last changes fastest.
Arguments:
- classes: int32 [128, 64, 128], P('gx', 'gy'), may hold values from 0 to 3
- support_mask: int32 [128, 64, 128], P('gx', 'gy'), may hold values from 1 to 255, as said below
Outputs:
- basis: float32 [8, 128, 64, 128], P(None, 'gx', 'gy')
- coarse_operator: float32 [27, 16, 16, 8], P(None, 'gx')
The draws below stay inside these ranges and needn't reach their ends.
Inputs may be any that keep to these rules, and one draw needn't show every extreme that they name: `support_mask`: bit c = 4 a + 2 b + e of a cell's entry is set when the cell lies in the support of its channel-c node; the bit of the channel whose node is the cell's own 8 x 8 x 8 block is always set.
All inputs are finite; a program needn't handle non-finite values.
Results may differ from the reference program's by a relative error of at most 0.0001.
Values sent between devices are 32-bit elements; how exact they have to be, the bound alone decides.
A program may use at most 64 MiB of HBM per device.

```python
import jax
import jax.numpy as jnp
from jax import lax

NZ = 128
ITERS = 2
NX = 128
NY = 64
NCX = 16
NCY = 8
NCZ = 16


def draw_support_mask(key, part):
    key = jax.random.fold_in(key, 11)
    reaches = jax.random.randint(key, (6, NX // 8, NY // 8, NZ // 8), 1, 4)
    counts = (NX, NY, NZ)
    result = jnp.zeros((NX, NY, NZ), jnp.int32)
    for channel in range(8):
        chosen = (channel // 4, channel // 2 % 2, channel % 2)
        nodes = []
        offsets = []
        for axis in range(3):
            places = jnp.arange(counts[axis], dtype=jnp.int32)
            blocks = places // 8
            node = jnp.where(blocks % 2 == chosen[axis], blocks, jnp.where(places % 8 < 4, blocks - 1, blocks + 1))
            nodes.append(node % (counts[axis] // 8))
            offsets.append(places - 8 * node)
        index_first = nodes[0][:, None, None]
        index_second = nodes[1][None, :, None]
        index_third = nodes[2][None, None, :]
        inside = jnp.ones((NX, NY, NZ), jnp.bool_)
        for axis in range(3):
            layout = [1, 1, 1]
            layout[axis] = counts[axis]
            offset = offsets[axis].reshape(layout)
            lower_reach = reaches[2 * axis][index_first, index_second, index_third]
            upper_reach = reaches[2 * axis + 1][index_first, index_second, index_third]
            inside = inside & (offset >= -lower_reach) & (offset <= 7 + upper_reach)
        result = result + inside.astype(jnp.int32) * 2 ** channel
    return result


def place_ends(entries, stream_key, smallest, largest):
    shape = entries.shape
    spot = [jax.random.randint(jax.random.fold_in(stream_key, axis), (), 0, shape[axis]) for axis in range(len(shape))]
    entries = entries.at[tuple(spot)].set(smallest)
    longest = shape.index(max(shape))
    spot[longest] = (spot[longest] + 1) % shape[longest]
    return entries.at[tuple(spot)].set(largest)


def setup_inputs(seed: int = 0) -> dict:
    keys = jax.random.split(jax.random.key(seed), 3)
    return {
        "classes": place_ends(jax.random.randint(keys[0], (NX, NY, NZ), 0, 4), jax.random.fold_in(keys[0], 1), 0, 3).astype(jnp.int32),
        "support_mask": draw_support_mask(jax.random.fold_in(keys[2], 71), 0),
    }


OMEGA = 2.0 / 3.0
COARSE_SCALE = 1.0 / 64.0
HIGHEST = lax.Precision.HIGHEST


def conduct(classes):
    return jnp.where(classes == 0, 0.01, jnp.where(classes == 1, 0.1, jnp.where(classes == 2, 1.0, 10.0))).astype(jnp.float32)


def harmonic(first, second):
    return 2.0 * first * second / (first + second)


def channel_bits(support):
    return jnp.stack([((support // (2 ** c)) % 2).astype(jnp.float32) for c in range(8)])


def axis_nodes(places, chosen):
    blocks = places // 8
    return jnp.where(blocks % 2 == chosen, blocks, jnp.where(places % 8 < 4, blocks - 1, blocks + 1))


def weights(places, chosen):
    nodes = axis_nodes(places, chosen)
    return 1.0 - jnp.abs(places.astype(jnp.float32) - 8.0 * nodes.astype(jnp.float32) - 3.5) / 8.0


def normalize(fields):
    return fields / jnp.sum(fields, axis=0, keepdims=True)


def start_fields(bits, first_pos, second_pos, third_pos):
    listed = []
    for c in range(8):
        along_first = weights(first_pos, c // 4)
        along_second = weights(second_pos, (c // 2) % 2)
        along_third = weights(third_pos, c % 2)
        listed.append(bits[c] * along_first[:, None, None] * along_second[None, :, None] * along_third[None, None, :])
    return normalize(jnp.stack(listed))


def faces(kappa):
    others = [jnp.roll(kappa, 1, 0), jnp.roll(kappa, -1, 0), jnp.roll(kappa, 1, 1),
              jnp.roll(kappa, -1, 1), jnp.roll(kappa, 1, 2), jnp.roll(kappa, -1, 2)]
    trans = tuple(harmonic(kappa, other) for other in others)
    diag = trans[0] + trans[1] + trans[2] + trans[3] + trans[4] + trans[5]
    return trans, diag


def neighbours(field, trans):
    west, east, south, north, below, above = trans
    return (west * jnp.roll(field, 1, 0) + east * jnp.roll(field, -1, 0) + south * jnp.roll(field, 1, 1)
            + north * jnp.roll(field, -1, 1) + below * jnp.roll(field, 1, 2) + above * jnp.roll(field, -1, 2))


def block_sum(product):
    chans, sx, sy, sz = product.shape
    return product.reshape(chans, sx // 4, 4, sy // 4, 4, sz // 4, 4).sum(axis=(2, 4, 6))


def axis_table(places, base, rows, own_bit, other_bit):
    node_own = axis_nodes(places, own_bit)
    node_other = axis_nodes(places, other_bit)
    row_index = (node_own - base) % rows
    lines = (row_index[:, None] == jnp.arange(rows, dtype=jnp.int32)[None, :]).astype(jnp.float32)
    offset = ((node_other - node_own + 1)[:, None] == jnp.arange(3, dtype=jnp.int32)[None, :]).astype(jnp.float32)
    return lines[:, :, None] * offset[:, None, :]


def pair_tables(places, base, rows, bit_shift):
    tables = {}
    for own_bit in (0, 1):
        for other_bit in (0, 1):
            tables[(own_bit, other_bit)] = axis_table(places, base, rows, own_bit, other_bit)
    return jnp.stack([tables[((c >> bit_shift) & 1, (d >> bit_shift) & 1)] for c in range(8) for d in range(8)])


def contract(sums, first_pos, first_base, first_rows, second_pos, second_base, second_rows, third_pos, third_rows):
    along_first = pair_tables(first_pos, first_base, first_rows, 2)
    along_second = pair_tables(second_pos, second_base, second_rows, 1)
    along_third = pair_tables(third_pos, 0, third_rows, 0)
    section_one = jnp.einsum('pxyz,pzkc->pxykc', sums, along_third, precision=HIGHEST)
    section_two = jnp.einsum('pxykc,pxia->piaykc', section_one, along_first, precision=HIGHEST)
    section_three = jnp.einsum('piaykc,pyjb->abcikj', section_two, along_second, precision=HIGHEST)
    return section_three.reshape(27, first_rows, third_rows, second_rows)


def reference(classes, support_mask):
    kappa = conduct(classes)
    trans, diag = faces(kappa)
    bits = channel_bits(support_mask)
    first_pos = jnp.arange(NX, dtype=jnp.int32)
    second_pos = jnp.arange(NY, dtype=jnp.int32)
    third_pos = jnp.arange(NZ, dtype=jnp.int32)
    fields = start_fields(bits, first_pos, second_pos, third_pos)
    for step in range(ITERS):
        near = lax.map(lambda field: neighbours(field, trans), fields)
        fields = normalize(bits * ((1.0 - OMEGA) * fields + OMEGA * near / diag))
    near = lax.map(lambda field: neighbours(field, trans), fields)
    images = diag * fields - near
    sums = lax.map(lambda field: block_sum(field[None] * images), fields)
    sums = sums.reshape(64, NX // 4, NY // 4, NZ // 4)
    quarter_first = 4 * jnp.arange(NX // 4, dtype=jnp.int32)
    quarter_second = 4 * jnp.arange(NY // 4, dtype=jnp.int32)
    quarter_third = 4 * jnp.arange(NZ // 4, dtype=jnp.int32)
    coarse = contract(sums, quarter_first, 0, NCX, quarter_second, 0, NCY, quarter_third, NCZ)
    return fields, coarse * COARSE_SCALE
```

```python
import functools

import jax
import jax.numpy as jnp
from jax import lax
from jax.experimental import pallas as pl
from jax.experimental.pallas import tpu as pltpu
from jax.sharding import PartitionSpec as P

COARSE_SCALE = 1.0 / 64.0
HALO = 3
EDGE = 8
MESH = pl.DeviceIdType.MESH


def node_of(places, chosen):
    blocks = places >> 3
    same = (blocks & 1) == chosen
    return jnp.where(same, blocks, jnp.where((places & 7) < 4, blocks - 1, blocks + 1))


def weight_of(places, chosen):
    distance = (places - 8 * node_of(places, chosen)).astype(jnp.float32) - 3.5
    return 1.0 - jnp.abs(distance) / 8.0


def harmonic(first, second):
    return 2.0 * first * second / (first + second)


def split_dot(left, right, left_is_table):
    data = right if left_is_table else left
    high = data.astype(jnp.bfloat16)
    low = (data - high.astype(jnp.float32)).astype(jnp.bfloat16)
    if left_is_table:
        return jnp.dot(left, high, preferred_element_type=jnp.float32) + jnp.dot(
            left, low, preferred_element_type=jnp.float32
        )
    return jnp.dot(high, right, preferred_element_type=jnp.float32) + jnp.dot(
        low, right, preferred_element_type=jnp.float32
    )


def kernel(
    nx,
    ny,
    cls_hbm,
    msk_hbm,
    basis_hbm,
    coarse_ref,
    cells,
    edge,
    sides,
    kappa,
    t_east,
    t_north,
    t_above,
    diag,
    plane_w,
    phi_a,
    phi_b,
    image,
    pairs,
    table_y,
    table_z,
    terms,
    to_low,
    to_high,
    to_own,
    from_low,
    from_high,
    from_own,
    load_sem,
    halo_send,
    halo_recv,
    term_send,
    term_recv,
    out_sem,
):
    width, rows, depth = cls_hbm.shape
    wide = rows + EDGE
    count_y = rows * ny // 8
    count_z = depth // 8
    gx, gy = lax.axis_index("gx"), lax.axis_index("gy")
    parity = lax.rem(gx, 2)
    own = pl.ds(HALO, width)
    main = pl.ds(0, rows)
    tail = pl.ds(rows, EDGE)

    def peer(dx, dy):
        return (lax.rem(gx + dx + nx, nx), lax.rem(gy + dy + ny, ny))

    loads = [
        pltpu.make_async_copy(ref, cells.at[i, own, main, :], load_sem.at[i])
        for i, ref in enumerate((cls_hbm, msk_hbm))
    ]
    for copy in loads:
        copy.start()

    partners = [(dx, dy) for dx in (-1, 0, 1) for dy in range(ny) if (dx, dy) != (0, 0)]
    barrier = pltpu.get_barrier_semaphore()
    for dx, dy in partners:
        pl.semaphore_signal(barrier, inc=1, device_id=peer(dx, dy), device_id_type=MESH)

    row_pos = lax.broadcasted_iota(jnp.int32, (wide, depth), 0)
    second = gy * rows + jnp.where(row_pos < rows + EDGE // 2, row_pos, row_pos - wide)
    third = lax.broadcasted_iota(jnp.int32, (wide, depth), 1)
    for b in (0, 1):
        for e in (0, 1):
            plane_w[2 * b + e] = weight_of(second, b) * weight_of(third, e)
    place = lax.broadcasted_iota(jnp.int32, (depth, 128), 0)
    lane = lax.broadcasted_iota(jnp.int32, (depth, 128), 1)
    for e in (0, 1):
        for other in (0, 1):
            mine = node_of(place, e)
            shift = node_of(place, other) - mine + 1
            column = lax.rem(mine + count_z, count_z) + count_z * shift
            table_z[pl.ds((2 * e + other) * depth, depth), :] = jnp.where(
                column == lane, 1.0, 0.0
            ).astype(jnp.bfloat16)
    line = lax.broadcasted_iota(jnp.int32, table_y.shape, 0)
    column = lax.broadcasted_iota(jnp.int32, table_y.shape, 1)
    bits = column // rows
    spot = gy * rows + column - rows * bits
    mine = jnp.where(bits >= 2, node_of(spot, 1), node_of(spot, 0))
    theirs = jnp.where((bits & 1) == 1, node_of(spot, 1), node_of(spot, 0))
    target = lax.rem(mine + count_y, count_y) + count_y * (theirs - mine + 1)
    table_y[...] = jnp.where(target == line, 1.0, 0.0).astype(jnp.bfloat16)

    for copy in loads:
        copy.wait()
    sub = lax.broadcasted_iota(jnp.int32, (width, EDGE, depth), 1)
    if ny == 2:
        for i in (0, 1):
            edge[i] = jnp.where(
                sub < EDGE // 2,
                cells[i, own, pl.ds(0, EDGE), :],
                cells[i, own, pl.ds(rows - EDGE, EDGE), :],
            )
    pl.semaphore_wait(barrier, len(partners))

    copies = {}

    def send(key, src, dst, dx, dy):
        index = len(copies)
        copies[key] = pltpu.make_async_remote_copy(
            src_ref=src,
            dst_ref=dst,
            send_sem=halo_send.at[index],
            recv_sem=halo_recv.at[index],
            device_id=peer(dx, dy),
            device_id_type=MESH,
        )
        copies[key].start()

    spans = {
        0: (0, HALO, width),
        -1: (0, HALO + width, HALO),
        1: (width - HALO, 0, HALO),
    }
    for dx in (1, -1):
        start, land, size = spans[dx]
        send(
            ("x", dx),
            cells.at[:, pl.ds(HALO + start, size), main, :],
            cells.at[:, pl.ds(land, size), main, :],
            dx,
            0,
        )
    for dx in (1, -1, 0):
        start, land, size = spans[dx]
        if dx == 0:
            land = HALO
        if ny == 2:
            send(
                ("y", dx, 0),
                edge.at[:, pl.ds(start, size), :, :],
                cells.at[:, pl.ds(land, size), tail, :],
                dx,
                1,
            )
        else:
            for side, dy, first in ((0, -1, 0), (1, 1, rows - EDGE)):
                send(
                    ("y", dx, side),
                    cells.at[:, pl.ds(HALO + start, size), pl.ds(first, EDGE), :],
                    sides.at[side, :, pl.ds(land, size), :, :],
                    dx,
                    dy,
                )

    def receive(dx):
        _, land, size = spans[dx]
        if dx == 0:
            land = HALO
        else:
            copies[("x", dx)].wait_recv()
        if ny == 2:
            copies[("y", dx, 0)].wait_recv()
        else:
            for side in (0, 1):
                copies[("y", dx, side)].wait_recv()
            part = lax.broadcasted_iota(jnp.int32, (size, EDGE, depth), 1)
            for i in (0, 1):
                cells[i, pl.ds(land, size), tail, :] = jnp.where(
                    part < EDGE // 2,
                    sides[0, i, pl.ds(land, size), :, :],
                    sides[1, i, pl.ds(land, size), :, :],
                )

    def up(plane, axis):
        return pltpu.roll(plane, 1, axis)

    def down(plane, axis):
        return pltpu.roll(plane, plane.shape[axis] - 1, axis)

    def prepare(x):
        classes = cells[0, x]
        mask = cells[1, x]
        k = jnp.where(
            classes == 0, 0.01, jnp.where(classes == 1, 0.1, jnp.where(classes == 2, 1.0, 10.0))
        ).astype(jnp.float32)
        kappa[x] = k
        t_north[x] = harmonic(k, down(k, 0))
        t_above[x] = harmonic(k, down(k, 1))
        at = jnp.full((1, depth), gx * width + x - HALO, jnp.int32)
        along = [weight_of(at, 0), weight_of(at, 1)]
        fields = []
        total = None
        for c in range(8):
            value = jnp.where((mask & (1 << c)) != 0, along[c // 4] * plane_w[c % 4], 0.0)
            fields.append(value)
            total = value if total is None else total + value
        scale = 1.0 / total
        for c in range(8):
            phi_a[c, x] = fields[c] * scale

    def join(x):
        t_east[x] = harmonic(kappa[x], kappa[x + 1])

    def gather(x):
        diag[x] = (
            t_east[x - 1]
            + t_east[x]
            + up(t_north[x], 0)
            + t_north[x]
            + up(t_above[x], 1)
            + t_above[x]
        )

    def near(source, c, x, coefs):
        west, east, south, north, below, above = coefs
        field = source[c, x]
        return field, (
            west * source[c, x - 1]
            + east * source[c, x + 1]
            + south * up(field, 0)
            + north * down(field, 0)
            + below * up(field, 1)
            + above * down(field, 1)
        )

    def coefficients(x):
        north, above = t_north[x], t_above[x]
        return (t_east[x - 1], t_east[x], up(north, 0), north, up(above, 1), above)

    def smooth(source, target, x):
        coefs = coefficients(x)
        half = 0.5 * diag[x]
        mask = cells[1, x]
        total = None
        for c in range(8):
            field, sums = near(source, c, x, coefs)
            value = jnp.where((mask & (1 << c)) != 0, half * field + sums, 0.0)
            target[c, x] = value
            total = value if total is None else total + value
        scale = 1.0 / total
        for c in range(8):
            target[c, x] = target[c, x] * scale

    def apply(source, x):
        coefs = coefficients(x)
        centre = diag[x]
        for d in range(8):
            field, sums = near(source, d, x, coefs)
            image[d, x - HALO] = (centre * field - sums)[:rows]

    def inner(work, first, last):
        def body(x, carry):
            work(x)
            return carry

        lax.fori_loop(first, last, body, 0)

    def outer(work, low, high, size=HALO):
        def body(i, carry):
            work(i + low + (i // size) * (high - low - size))
            return carry

        lax.fori_loop(0, 2 * size, body, 0)

    top = HALO + width
    receive(0)
    inner(prepare, HALO, top)
    inner(join, HALO, top - 1)
    inner(gather, HALO + 1, top - 1)
    inner(functools.partial(smooth, phi_a, phi_b), HALO + 1, top - 1)

    receive(1)
    receive(-1)
    outer(prepare, 0, top)
    outer(join, 0, top - 1)
    outer(gather, 1, top - 1)
    outer(functools.partial(smooth, phi_a, phi_b), 1, top - 1)
    inner(functools.partial(smooth, phi_b, phi_a), HALO - 1, top + 1)
    stored = pltpu.make_async_copy(phi_a.at[:, own, main, :], basis_hbm, out_sem)
    stored.start()
    inner(functools.partial(apply, phi_a), HALO, top)

    tiles = rows // 8

    def products(step, carry):
        half = step // tiles
        tile = pl.multiple_of(lax.rem(step, tiles) * 8, 8)
        at = pl.ds(tile, 8)
        for c_half in range(2):
            total = {}
            for i in range(width // 2):
                x = half * (width // 2) + i
                images = [image[d, x, at, :] for d in range(8)]
                for c in range(4 * c_half, 4 * c_half + 4):
                    field = phi_a[c, x + HALO, at, :]
                    for d in range(8):
                        value = field * images[d]
                        total[c, d] = value if i == 0 else total[c, d] + value
            for (c, d), value in total.items():
                group = ((c >> 2) * 2 + (d >> 2)) * 2 + half
                block = (c >> 1 & 1) * 2 + (d >> 1 & 1)
                column = (c & 1) * 2 + (d & 1)
                pairs[group, pl.ds(block * rows + tile, 8), pl.ds(column * depth, depth)] = value
        return carry

    lax.fori_loop(0, 2 * tiles, products, 0)

    for group in range(8):
        section = split_dot(pairs[group], table_z[...], False)
        terms[group] = split_dot(table_y[...], section, True)

    def term(a, other, half):
        return terms[(a * 2 + other) * 2 + half]

    mine, off = parity, 1 - parity
    to_low[0] = term(off, off, 0)
    to_low[1] = term(off, mine, 0)
    to_high[0] = term(off, off, 1)
    to_high[1] = term(off, mine, 1)
    to_own[0] = term(mine, off, 0)
    to_own[1] = term(mine, mine, 0) + term(mine, mine, 1)
    to_own[2] = term(mine, off, 1)

    sent = []
    for source, landing, dx in ((to_low, from_high, -1), (to_high, from_low, 1), (to_own, from_own, 0)):
        for dy in range(ny):
            if (dx, dy) == (0, 0):
                continue
            index = len(sent)
            copy = pltpu.make_async_remote_copy(
                src_ref=source,
                dst_ref=landing.at[dy],
                send_sem=term_send.at[index],
                recv_sem=term_recv.at[index],
                device_id=peer(dx, dy),
                device_id_type=MESH,
            )
            copy.start()
            sent.append(copy)
    for copy in sent:
        copy.wait_recv()

    before = [to_own[0], to_own[1], to_own[2]]
    for dy in range(ny):
        if dy:
            before = [before[i] + from_own[dy, i] for i in range(3)]
        before[0] = before[0] + from_low[dy, 1]
        before[1] = before[1] + from_low[dy, 0] + from_high[dy, 0]
        before[2] = before[2] + from_high[dy, 1]
    for xo in range(3):
        tile = before[xo] * COARSE_SCALE
        short = 128 - tile.shape[0]
        if short:
            tile = jnp.concatenate([tile, jnp.zeros((short, 128), jnp.float32)], axis=0)
        turned = tile.T
        for yo in range(3):
            for zo in range(3):
                coarse_ref[9 * xo + 3 * yo + zo, 0] = turned[
                    zo * count_z : (zo + 1) * count_z, yo * count_y : (yo + 1) * count_y
                ]

    for copy in copies.values():
        copy.wait_send()
    for copy in sent:
        copy.wait_send()
    stored.wait()


def shards(classes, support_mask):
    nx, ny = lax.axis_size("gx"), lax.axis_size("gy")
    width, rows, depth = classes.shape
    wide, deep = rows + EDGE, width + 2 * HALO
    count_y, count_z = rows * ny // 8, depth // 8
    lines = 3 * count_y
    partners = 3 * ny - 1
    halos = 5 if ny == 2 else 8
    plane = lambda *lead: pltpu.VMEM((*lead, wide, depth), jnp.float32)
    return pl.pallas_call(
        functools.partial(kernel, nx, ny),
        out_shape=(
            jax.ShapeDtypeStruct((8, width, rows, depth), jnp.float32),
            jax.ShapeDtypeStruct((27, 1, count_z, count_y), jnp.float32),
        ),
        in_specs=[pl.BlockSpec(memory_space=pl.ANY)] * 2,
        out_specs=(
            pl.BlockSpec(memory_space=pl.ANY),
            pl.BlockSpec(memory_space=pltpu.VMEM),
        ),
        scratch_shapes=[
            pltpu.VMEM((2, deep, wide, depth), jnp.int32),
            pltpu.VMEM((2, width, EDGE, depth), jnp.int32),
            pltpu.VMEM((2, 2, deep, EDGE, depth) if ny > 2 else (1, 1, 1, EDGE, depth), jnp.int32),
            plane(deep),
            plane(deep),
            plane(deep),
            plane(deep),
            plane(deep),
            plane(4),
            plane(8, deep),
            plane(8, deep),
            pltpu.VMEM((8, width, rows, depth), jnp.float32),
            pltpu.VMEM((8, 4 * rows, 4 * depth), jnp.float32),
            pltpu.VMEM((lines, 4 * rows), jnp.bfloat16),
            pltpu.VMEM((4 * depth, 128), jnp.bfloat16),
            pltpu.VMEM((8, lines, 128), jnp.float32),
            pltpu.VMEM((2, lines, 128), jnp.float32),
            pltpu.VMEM((2, lines, 128), jnp.float32),
            pltpu.VMEM((3, lines, 128), jnp.float32),
            pltpu.VMEM((ny, 2, lines, 128), jnp.float32),
            pltpu.VMEM((ny, 2, lines, 128), jnp.float32),
            pltpu.VMEM((ny, 3, lines, 128), jnp.float32),
            pltpu.SemaphoreType.DMA((2,)),
            pltpu.SemaphoreType.DMA((halos,)),
            pltpu.SemaphoreType.DMA((halos,)),
            pltpu.SemaphoreType.DMA((partners,)),
            pltpu.SemaphoreType.DMA((partners,)),
            pltpu.SemaphoreType.DMA,
        ],
        compiler_params=pltpu.CompilerParams(
            collective_id=0, has_side_effects=True, vmem_limit_bytes=32 * 1024 * 1024
        ),
    )(classes, support_mask)


def solution(mesh):
    in_specs = (P("gx", "gy", None), P("gx", "gy", None))
    out_specs = (P(None, "gx", "gy", None), P(None, "gx", None, None))
    return jax.shard_map(shards, mesh=mesh, in_specs=in_specs, out_specs=out_specs, check_vma=False)
```

```python
import functools

import jax
import jax.numpy as jnp
from jax import lax
from jax.experimental import pallas as pl
from jax.experimental.pallas import tpu as pltpu
from jax.sharding import PartitionSpec as P

COARSE_SCALE = 1.0 / 64.0
HALO = 3
EDGE = 8
MESH = pl.DeviceIdType.MESH


def node_of(places, chosen):
    blocks = places >> 3
    same = (blocks & 1) == chosen
    return jnp.where(same, blocks, jnp.where((places & 7) < 4, blocks - 1, blocks + 1))


def wrap(node, count):
    return jnp.where(node < 0, node + count, jnp.where(node >= count, node - count, node))


def weight_of(places, chosen):
    distance = (places - 8 * node_of(places, chosen)).astype(jnp.float32) - 3.5
    return 1.0 - jnp.abs(distance) / 8.0


def harmonic(first, second):
    return 2.0 * first * second / (first + second)


def split_dot(left, right, left_is_table):
    data = right if left_is_table else left
    high = data.astype(jnp.bfloat16)
    low = (data - high.astype(jnp.float32)).astype(jnp.bfloat16)
    if left_is_table:
        return jnp.dot(left, high, preferred_element_type=jnp.float32) + jnp.dot(
            left, low, preferred_element_type=jnp.float32
        )
    return jnp.dot(high, right, preferred_element_type=jnp.float32) + jnp.dot(
        low, right, preferred_element_type=jnp.float32
    )


def kernel(
    nx,
    ny,
    both_hbm,
    basis_hbm,
    coarse_ref,
    cells,
    edge,
    sides,
    kappa,
    t_east,
    t_north,
    t_above,
    diag,
    plane_w,
    phi_a,
    phi_b,
    image,
    pairs,
    table_y,
    table_z,
    terms,
    to_low,
    to_high,
    to_own,
    from_low,
    from_high,
    from_own,
    load_sem,
    halo_send,
    halo_recv,
    term_send,
    term_recv,
    out_sem,
):
    _, width, rows, depth = both_hbm.shape
    wide = rows + EDGE
    count_y = rows * ny // 8
    count_z = depth // 8
    gx, gy = lax.axis_index("gx"), lax.axis_index("gy")
    parity = lax.rem(gx, 2)
    own = pl.ds(HALO, width)
    main = pl.ds(0, rows)
    tail = pl.ds(rows, EDGE)

    def peer(dx, dy):
        return (lax.rem(gx + dx + nx, nx), lax.rem(gy + dy + ny, ny))

    loads = [pltpu.make_async_copy(both_hbm, cells.at[:, own, main, :], load_sem.at[0])]
    for copy in loads:
        copy.start()

    partners = [(dx, dy) for dx in (-1, 0, 1) for dy in range(ny) if (dx, dy) != (0, 0)]
    barrier = pltpu.get_barrier_semaphore()
    for dx, dy in partners:
        pl.semaphore_signal(barrier, inc=1, device_id=peer(dx, dy), device_id_type=MESH)

    for copy in loads:
        copy.wait()
    sub = lax.broadcasted_iota(jnp.int32, (width, EDGE, depth), 1)
    if ny == 2:
        for i in (0, 1):
            edge[i] = jnp.where(
                sub < EDGE // 2,
                cells[i, own, pl.ds(0, EDGE), :],
                cells[i, own, pl.ds(rows - EDGE, EDGE), :],
            )
    pl.semaphore_wait(barrier, len(partners))

    copies = {}

    def send(key, src, dst, dx, dy):
        index = len(copies)
        copies[key] = pltpu.make_async_remote_copy(
            src_ref=src,
            dst_ref=dst,
            send_sem=halo_send.at[index],
            recv_sem=halo_recv.at[index],
            device_id=peer(dx, dy),
            device_id_type=MESH,
        )
        copies[key].start()

    spans = {
        0: (0, HALO, width),
        -1: (0, HALO + width, HALO),
        1: (width - HALO, 0, HALO),
    }
    for i in (0, 1):
        for p in range(HALO):
            for dx in (1, -1):
                start, land, size = spans[dx]
                send(
                    ("x", dx, i, p),
                    cells.at[i, HALO + start + p, main, :],
                    cells.at[i, land + p, main, :],
                    dx,
                    0,
                )
    for dx in (1, -1, 0):
        start, land, size = spans[dx]
        if dx == 0:
            land = HALO
        if ny == 2:
            send(
                ("y", dx, 0),
                edge.at[:, pl.ds(start, size), :, :],
                cells.at[:, pl.ds(land, size), tail, :],
                dx,
                1,
            )
        else:
            for side, dy, first in ((0, -1, 0), (1, 1, rows - EDGE)):
                send(
                    ("y", dx, side),
                    cells.at[:, pl.ds(HALO + start, size), pl.ds(first, EDGE), :],
                    sides.at[side, :, pl.ds(land, size), :, :],
                    dx,
                    dy,
                )

    row_pos = lax.broadcasted_iota(jnp.int32, (wide, depth), 0)
    second = gy * rows + jnp.where(row_pos < rows + EDGE // 2, row_pos, row_pos - wide)
    third = lax.broadcasted_iota(jnp.int32, (wide, depth), 1)
    for b in (0, 1):
        for e in (0, 1):
            plane_w[2 * b + e] = weight_of(second, b) * weight_of(third, e)
    place = lax.broadcasted_iota(jnp.int32, (depth, 128), 0)
    lane = lax.broadcasted_iota(jnp.int32, (depth, 128), 1)
    for e in (0, 1):
        for other in (0, 1):
            mine = node_of(place, e)
            shift = node_of(place, other) - mine + 1
            column = wrap(mine, count_z) + count_z * shift
            table_z[pl.ds((2 * e + other) * depth, depth), :] = jnp.where(
                column == lane, 1.0, 0.0
            ).astype(jnp.bfloat16)
    line = lax.broadcasted_iota(jnp.int32, table_y.shape, 0)
    column = lax.broadcasted_iota(jnp.int32, table_y.shape, 1)
    bits = column // rows
    spot = gy * rows + column - rows * bits
    mine = jnp.where(bits >= 2, node_of(spot, 1), node_of(spot, 0))
    theirs = jnp.where((bits & 1) == 1, node_of(spot, 1), node_of(spot, 0))
    target = wrap(mine, count_y) + count_y * (theirs - mine + 1)
    table_y[...] = jnp.where(target == line, 1.0, 0.0).astype(jnp.bfloat16)

    def receive(dx):
        _, land, size = spans[dx]
        if dx == 0:
            land = HALO
        else:
            for i in (0, 1):
                for p in range(HALO):
                    copies[("x", dx, i, p)].wait_recv()
        if ny == 2:
            copies[("y", dx, 0)].wait_recv()
        else:
            for side in (0, 1):
                copies[("y", dx, side)].wait_recv()
            part = lax.broadcasted_iota(jnp.int32, (size, EDGE, depth), 1)
            for i in (0, 1):
                cells[i, pl.ds(land, size), tail, :] = jnp.where(
                    part < EDGE // 2,
                    sides[0, i, pl.ds(land, size), :, :],
                    sides[1, i, pl.ds(land, size), :, :],
                )

    def up(plane, axis):
        return pltpu.roll(plane, 1, axis)

    def down(plane, axis):
        return pltpu.roll(plane, plane.shape[axis] - 1, axis)

    def prepare(x):
        classes = cells[0, x]
        mask = cells[1, x]
        k = jnp.where(
            classes == 0, 0.01, jnp.where(classes == 1, 0.1, jnp.where(classes == 2, 1.0, 10.0))
        ).astype(jnp.float32)
        kappa[x] = k
        t_north[x] = harmonic(k, down(k, 0))
        t_above[x] = harmonic(k, down(k, 1))
        at = jnp.full((1, depth), gx * width + x - HALO, jnp.int32)
        along = [weight_of(at, 0), weight_of(at, 1)]
        fields = []
        total = None
        for c in range(8):
            value = jnp.where((mask & (1 << c)) != 0, along[c // 4] * plane_w[c % 4], 0.0)
            fields.append(value)
            total = value if total is None else total + value
        scale = 1.0 / total
        for c in range(8):
            phi_a[c, x] = fields[c] * scale

    def join(x):
        t_east[x] = harmonic(kappa[x], kappa[x + 1])

    def gather(x):
        diag[x] = (
            t_east[x - 1]
            + t_east[x]
            + up(t_north[x], 0)
            + t_north[x]
            + up(t_above[x], 1)
            + t_above[x]
        )

    def near(source, c, x, coefs):
        west, east, south, north, below, above = coefs
        field = source[c, x]
        return field, (
            west * source[c, x - 1]
            + east * source[c, x + 1]
            + south * up(field, 0)
            + north * down(field, 0)
            + below * up(field, 1)
            + above * down(field, 1)
        )

    def coefficients(x):
        north, above = t_north[x], t_above[x]
        return (t_east[x - 1], t_east[x], up(north, 0), north, up(above, 1), above)

    def smooth(source, target, x):
        coefs = coefficients(x)
        half = 0.5 * diag[x]
        mask = cells[1, x]
        total = None
        for c in range(8):
            field, sums = near(source, c, x, coefs)
            value = jnp.where((mask & (1 << c)) != 0, half * field + sums, 0.0)
            target[c, x] = value
            total = value if total is None else total + value
        scale = 1.0 / total
        for c in range(8):
            target[c, x] = target[c, x] * scale

    def apply(source, x):
        coefs = coefficients(x)
        centre = diag[x]
        for d in range(8):
            field, sums = near(source, d, x, coefs)
            image[d, x - HALO] = (centre * field - sums)[:rows]

    def inner(work, first, last):
        def body(x, carry):
            work(x)
            return carry

        lax.fori_loop(first, last, body, 0, unroll=2)

    def beside(work, low, high, upper):
        def body(i, carry):
            work(i + low + upper * (high - low))
            return carry

        lax.fori_loop(0, HALO, body, 0, unroll=True)

    top = HALO + width
    first_step = functools.partial(smooth, phi_a, phi_b)
    second_step = functools.partial(smooth, phi_b, phi_a)
    operator = functools.partial(apply, phi_a)
    receive(0)
    inner(prepare, HALO, top)
    inner(join, HALO, top - 1)
    inner(gather, HALO + 1, top - 1)
    inner(first_step, HALO + 1, top - 1)
    inner(second_step, HALO + 2, top - 2)
    inner(operator, HALO + 3, top - 3)

    tiles = rows // 8

    def products(half):
        def body(step, carry):
            tile = pl.multiple_of(step * 8, 8)
            at = pl.ds(tile, 8)
            for c_half in range(2):
                total = {}
                for i in range(width // 2):
                    x = half * (width // 2) + i
                    images = [image[d, x, at, :] for d in range(8)]
                    for c in range(4 * c_half, 4 * c_half + 4):
                        field = phi_a[c, x + HALO, at, :]
                        for d in range(8):
                            value = field * images[d]
                            total[c, d] = value if i == 0 else total[c, d] + value
                for (c, d), value in total.items():
                    group = (c >> 2) * 2 + (d >> 2)
                    block = group * 4 + (c >> 1 & 1) * 2 + (d >> 1 & 1)
                    column = (c & 1) * 2 + (d & 1)
                    pairs[pl.ds(block * rows + tile, 8), pl.ds(column * depth, depth)] = value
            return carry

        lax.fori_loop(0, tiles, body, 0)
        section = split_dot(pairs[...], table_z[...], False)
        for group in range(4):
            part = section[group * 4 * rows : (group + 1) * 4 * rows]
            terms[half, group] = split_dot(table_y[...], part, True)

    for upper in (1 - parity, parity):
        @pl.when(upper == 1)
        def _():
            receive(-1)

        @pl.when(upper == 0)
        def _():
            receive(1)

        beside(prepare, 0, top, upper)
        beside(join, 0, top - 1, upper)
        beside(gather, 1, top - 1, upper)
        beside(first_step, 1, top - 1, upper)
        beside(second_step, 2, top - 2, upper)
        beside(operator, 3, top - 3, upper)
        products(upper)

    stored = pltpu.make_async_copy(phi_a.at[:, own, main, :], basis_hbm, out_sem)
    stored.start()

    def term(a, other, half):
        return terms[half, a * 2 + other]

    mine, off = parity, 1 - parity
    to_low[...] = term(off, off, 0) + pltpu.roll(term(off, mine, 0), 64, 1)
    to_high[...] = term(off, off, 1) + pltpu.roll(term(off, mine, 1), 64, 1)
    to_own[0] = term(mine, off, 0)
    to_own[1] = term(mine, mine, 0) + term(mine, mine, 1)
    to_own[2] = term(mine, off, 1)

    sent = []
    for source, landing, dx in ((to_low, from_high, -1), (to_high, from_low, 1), (to_own, from_own, 0)):
        for dy in range(ny):
            if (dx, dy) == (0, 0):
                continue
            index = len(sent)
            copy = pltpu.make_async_remote_copy(
                src_ref=source,
                dst_ref=landing.at[dy],
                send_sem=term_send.at[index],
                recv_sem=term_recv.at[index],
                device_id=peer(dx, dy),
                device_id_type=MESH,
            )
            copy.start()
            sent.append(copy)
    for copy in sent:
        copy.wait_recv()

    before = [to_own[0], to_own[1], to_own[2]]
    for dy in range(ny):
        if dy:
            before = [before[i] + from_own[dy, i] for i in range(3)]
        before[0] = before[0] + pltpu.roll(from_low[dy], 64, 1)
        before[1] = before[1] + from_low[dy] + from_high[dy]
        before[2] = before[2] + pltpu.roll(from_high[dy], 64, 1)
    for xo in range(3):
        tile = before[xo] * COARSE_SCALE
        short = 128 - tile.shape[0]
        if short:
            tile = jnp.concatenate([tile, jnp.zeros((short, 128), jnp.float32)], axis=0)
        turned = tile.T
        for yo in range(3):
            for zo in range(3):
                coarse_ref[9 * xo + 3 * yo + zo, 0] = turned[
                    zo * count_z : (zo + 1) * count_z, yo * count_y : (yo + 1) * count_y
                ]

    for copy in copies.values():
        copy.wait_send()
    for copy in sent:
        copy.wait_send()
    stored.wait()


def shards(classes, support_mask):
    nx, ny = lax.axis_size("gx"), lax.axis_size("gy")
    width, rows, depth = classes.shape
    wide, deep = rows + EDGE, width + 2 * HALO
    count_y, count_z = rows * ny // 8, depth // 8
    lines = 3 * count_y
    partners = 3 * ny - 1
    halos = 4 * HALO + (3 if ny == 2 else 6)
    plane = lambda *lead: pltpu.VMEM((*lead, wide, depth), jnp.float32)
    return pl.pallas_call(
        functools.partial(kernel, nx, ny),
        out_shape=(
            jax.ShapeDtypeStruct((8, width, rows, depth), jnp.float32),
            jax.ShapeDtypeStruct((27, 1, count_z, count_y), jnp.float32),
        ),
        in_specs=[pl.BlockSpec(memory_space=pl.ANY)],
        out_specs=(
            pl.BlockSpec(memory_space=pl.ANY),
            pl.BlockSpec(memory_space=pltpu.VMEM),
        ),
        scratch_shapes=[
            pltpu.VMEM((2, deep, wide, depth), jnp.int32),
            pltpu.VMEM((2, width, EDGE, depth), jnp.int32),
            pltpu.VMEM((2, 2, deep, EDGE, depth) if ny > 2 else (1, 1, 1, EDGE, depth), jnp.int32),
            plane(deep),
            plane(deep),
            plane(deep),
            plane(deep),
            plane(deep),
            plane(4),
            plane(8, deep),
            plane(8, deep),
            pltpu.VMEM((8, width, rows, depth), jnp.float32),
            pltpu.VMEM((16 * rows, 4 * depth), jnp.float32),
            pltpu.VMEM((lines, 4 * rows), jnp.bfloat16),
            pltpu.VMEM((4 * depth, 128), jnp.bfloat16),
            pltpu.VMEM((2, 4, lines, 128), jnp.float32),
            pltpu.VMEM((lines, 128), jnp.float32),
            pltpu.VMEM((lines, 128), jnp.float32),
            pltpu.VMEM((3, lines, 128), jnp.float32),
            pltpu.VMEM((ny, lines, 128), jnp.float32),
            pltpu.VMEM((ny, lines, 128), jnp.float32),
            pltpu.VMEM((ny, 3, lines, 128), jnp.float32),
            pltpu.SemaphoreType.DMA((2,)),
            pltpu.SemaphoreType.DMA((halos,)),
            pltpu.SemaphoreType.DMA((halos,)),
            pltpu.SemaphoreType.DMA((partners,)),
            pltpu.SemaphoreType.DMA((partners,)),
            pltpu.SemaphoreType.DMA,
        ],
        compiler_params=pltpu.CompilerParams(
            collective_id=0, has_side_effects=True, vmem_limit_bytes=32 * 1024 * 1024
        ),
    )(jnp.stack([classes, support_mask]))


def solution(mesh):
    in_specs = (P("gx", "gy", None), P("gx", "gy", None))
    out_specs = (P(None, "gx", "gy", None), P(None, "gx", None, None))
    return jax.shard_map(shards, mesh=mesh, in_specs=in_specs, out_specs=out_specs, check_vma=False)
```

```python
import functools

import jax
import jax.numpy as jnp
from jax import lax
from jax.experimental import pallas as pl
from jax.experimental.pallas import tpu as pltpu
from jax.sharding import PartitionSpec as P

COARSE_SCALE = 1.0 / 64.0
HALO = 3
EDGE = 8
MESH = pl.DeviceIdType.MESH


def node_of(places, chosen):
    blocks = places >> 3
    same = (blocks & 1) == chosen
    return jnp.where(same, blocks, jnp.where((places & 7) < 4, blocks - 1, blocks + 1))


def wrap(node, count):
    return jnp.where(node < 0, node + count, jnp.where(node >= count, node - count, node))


def weight_of(places, chosen):
    distance = (places - 8 * node_of(places, chosen)).astype(jnp.float32) - 3.5
    return 1.0 - jnp.abs(distance) / 8.0


def harmonic(first, second):
    return 2.0 * first * second / (first + second)


def split_dot(left, right, left_is_table):
    data = right if left_is_table else left
    high = data.astype(jnp.bfloat16)
    low = (data - high.astype(jnp.float32)).astype(jnp.bfloat16)
    if left_is_table:
        return jnp.dot(left, high, preferred_element_type=jnp.float32) + jnp.dot(
            left, low, preferred_element_type=jnp.float32
        )
    return jnp.dot(high, right, preferred_element_type=jnp.float32) + jnp.dot(
        low, right, preferred_element_type=jnp.float32
    )


def kernel(
    nx,
    ny,
    both_hbm,
    basis_hbm,
    coarse_ref,
    cells,
    edge,
    sides,
    kappa,
    t_east,
    t_north,
    t_above,
    diag,
    plane_w,
    phi_a,
    phi_b,
    image,
    pairs,
    table_y,
    table_z,
    terms,
    to_low,
    to_high,
    to_own,
    from_low,
    from_high,
    from_own,
    load_sem,
    halo_send,
    halo_recv,
    term_send,
    term_recv,
    out_sem,
):
    _, width, rows, depth = both_hbm.shape
    wide = rows + EDGE
    count_y = rows * ny // 8
    count_z = depth // 8
    gx, gy = lax.axis_index("gx"), lax.axis_index("gy")
    parity = lax.rem(gx, 2)
    own = pl.ds(HALO, width)
    main = pl.ds(0, rows)
    tail = pl.ds(rows, EDGE)

    def peer(dx, dy):
        return (lax.rem(gx + dx + nx, nx), lax.rem(gy + dy + ny, ny))

    loads = [pltpu.make_async_copy(both_hbm, cells.at[:, own, main, :], load_sem.at[0])]
    for copy in loads:
        copy.start()

    partners = [(dx, dy) for dx in (-1, 0, 1) for dy in range(ny) if (dx, dy) != (0, 0)]
    barrier = pltpu.get_barrier_semaphore()
    for dx, dy in partners:
        pl.semaphore_signal(barrier, inc=1, device_id=peer(dx, dy), device_id_type=MESH)

    for copy in loads:
        copy.wait()
    sub = lax.broadcasted_iota(jnp.int32, (width, EDGE, depth), 1)
    if ny == 2:
        for i in (0, 1):
            edge[i] = jnp.where(
                sub < EDGE // 2,
                cells[i, own, pl.ds(0, EDGE), :],
                cells[i, own, pl.ds(rows - EDGE, EDGE), :],
            )
    pl.semaphore_wait(barrier, len(partners))

    copies = {}

    def send(key, src, dst, dx, dy):
        index = len(copies)
        copies[key] = pltpu.make_async_remote_copy(
            src_ref=src,
            dst_ref=dst,
            send_sem=halo_send.at[index],
            recv_sem=halo_recv.at[index],
            device_id=peer(dx, dy),
            device_id_type=MESH,
        )
        copies[key].start()

    spans = {
        0: (0, HALO, width),
        -1: (0, HALO + width, HALO),
        1: (width - HALO, 0, HALO),
    }
    for i in (0, 1):
        for p in range(HALO):
            for dx in (1, -1):
                start, land, size = spans[dx]
                send(
                    ("x", dx, i, p),
                    cells.at[i, HALO + start + p, main, :],
                    cells.at[i, land + p, main, :],
                    dx,
                    0,
                )
    for dx in (1, -1, 0):
        start, land, size = spans[dx]
        if dx == 0:
            land = HALO
        if ny == 2:
            send(
                ("y", dx, 0),
                edge.at[:, pl.ds(start, size), :, :],
                cells.at[:, pl.ds(land, size), tail, :],
                dx,
                1,
            )
        else:
            for side, dy, first in ((0, -1, 0), (1, 1, rows - EDGE)):
                send(
                    ("y", dx, side),
                    cells.at[:, pl.ds(HALO + start, size), pl.ds(first, EDGE), :],
                    sides.at[side, :, pl.ds(land, size), :, :],
                    dx,
                    dy,
                )

    row_pos = lax.broadcasted_iota(jnp.int32, (wide, depth), 0)
    second = gy * rows + jnp.where(row_pos < rows + EDGE // 2, row_pos, row_pos - wide)
    third = lax.broadcasted_iota(jnp.int32, (wide, depth), 1)
    for b in (0, 1):
        for e in (0, 1):
            plane_w[2 * b + e] = weight_of(second, b) * weight_of(third, e)
    place = lax.broadcasted_iota(jnp.int32, (depth, 128), 0)
    lane = lax.broadcasted_iota(jnp.int32, (depth, 128), 1)
    for e in (0, 1):
        for other in (0, 1):
            mine = node_of(place, e)
            shift = node_of(place, other) - mine + 1
            column = wrap(mine, count_z) + count_z * shift
            table_z[pl.ds((2 * e + other) * depth, depth), :] = jnp.where(
                column == lane, 1.0, 0.0
            ).astype(jnp.bfloat16)
    line = lax.broadcasted_iota(jnp.int32, table_y.shape, 0)
    column = lax.broadcasted_iota(jnp.int32, table_y.shape, 1)
    bits = column // rows
    spot = gy * rows + column - rows * bits
    mine = jnp.where(bits >= 2, node_of(spot, 1), node_of(spot, 0))
    theirs = jnp.where((bits & 1) == 1, node_of(spot, 1), node_of(spot, 0))
    target = wrap(mine, count_y) + count_y * (theirs - mine + 1)
    table_y[...] = jnp.where(target == line, 1.0, 0.0).astype(jnp.bfloat16)

    def receive(dx):
        _, land, size = spans[dx]
        if dx == 0:
            land = HALO
        else:
            for i in (0, 1):
                for p in range(HALO):
                    copies[("x", dx, i, p)].wait_recv()
        if ny == 2:
            copies[("y", dx, 0)].wait_recv()
        else:
            for side in (0, 1):
                copies[("y", dx, side)].wait_recv()
            part = lax.broadcasted_iota(jnp.int32, (size, EDGE, depth), 1)
            for i in (0, 1):
                cells[i, pl.ds(land, size), tail, :] = jnp.where(
                    part < EDGE // 2,
                    sides[0, i, pl.ds(land, size), :, :],
                    sides[1, i, pl.ds(land, size), :, :],
                )

    def up(plane, axis):
        return pltpu.roll(plane, 1, axis)

    def down(plane, axis):
        return pltpu.roll(plane, plane.shape[axis] - 1, axis)

    def prepare(x):
        classes = cells[0, x]
        mask = cells[1, x]
        k = jnp.where(
            classes == 0, 0.01, jnp.where(classes == 1, 0.1, jnp.where(classes == 2, 1.0, 10.0))
        ).astype(jnp.float32)
        kappa[x] = k
        t_north[x] = harmonic(k, down(k, 0))
        t_above[x] = harmonic(k, down(k, 1))
        at = jnp.full((1, depth), gx * width + x - HALO, jnp.int32)
        along = [weight_of(at, 0), weight_of(at, 1)]
        fields = []
        total = None
        for c in range(8):
            value = jnp.where((mask & (1 << c)) != 0, along[c // 4] * plane_w[c % 4], 0.0)
            fields.append(value)
            total = value if total is None else total + value
        scale = 1.0 / total
        for c in range(8):
            phi_a[c, x] = fields[c] * scale

    def join(x):
        t_east[x] = harmonic(kappa[x], kappa[x + 1])

    def gather(x):
        diag[x] = (
            t_east[x - 1]
            + t_east[x]
            + up(t_north[x], 0)
            + t_north[x]
            + up(t_above[x], 1)
            + t_above[x]
        )

    def near(source, c, x, coefs):
        west, east, south, north, below, above = coefs
        field = source[c, x]
        return field, (
            west * source[c, x - 1]
            + east * source[c, x + 1]
            + south * up(field, 0)
            + north * down(field, 0)
            + below * up(field, 1)
            + above * down(field, 1)
        )

    def coefficients(x):
        north, above = t_north[x], t_above[x]
        return (t_east[x - 1], t_east[x], up(north, 0), north, up(above, 1), above)

    def smooth(source, target, x):
        coefs = coefficients(x)
        half = 0.5 * diag[x]
        mask = cells[1, x]
        total = None
        for c in range(8):
            field, sums = near(source, c, x, coefs)
            value = jnp.where((mask & (1 << c)) != 0, half * field + sums, 0.0)
            target[c, x] = value
            total = value if total is None else total + value
        scale = 1.0 / total
        for c in range(8):
            target[c, x] = target[c, x] * scale

    def apply(source, x):
        coefs = coefficients(x)
        centre = diag[x]
        for d in range(8):
            field, sums = near(source, d, x, coefs)
            image[d, x - HALO] = (centre * field - sums)[:rows]

    def inner(work, first, last):
        def body(x, carry):
            work(x)
            return carry

        lax.fori_loop(first, last, body, 0, unroll=2)

    def beside(work, low, high, upper):
        def body(i, carry):
            work(i + low + upper * (high - low))
            return carry

        lax.fori_loop(0, HALO, body, 0, unroll=True)

    top = HALO + width
    first_step = functools.partial(smooth, phi_a, phi_b)
    second_step = functools.partial(smooth, phi_b, phi_a)
    operator = functools.partial(apply, phi_a)
    receive(0)
    inner(prepare, HALO, top)
    inner(join, HALO, top - 1)
    inner(gather, HALO + 1, top - 1)
    inner(first_step, HALO + 1, top - 1)
    inner(second_step, HALO + 2, top - 2)
    inner(operator, HALO + 3, top - 3)

    tiles = rows // 8

    def products(half):
        def body(step, carry):
            tile = pl.multiple_of(step * 8, 8)
            at = pl.ds(tile, 8)
            for c_half in range(2):
                total = {}
                for i in range(width // 2):
                    x = half * (width // 2) + i
                    images = [image[d, x, at, :] for d in range(8)]
                    for c in range(4 * c_half, 4 * c_half + 4):
                        field = phi_a[c, x + HALO, at, :]
                        for d in range(8):
                            value = field * images[d]
                            total[c, d] = value if i == 0 else total[c, d] + value
                for (c, d), value in total.items():
                    group = (c >> 2) * 2 + (d >> 2)
                    block = group * 4 + (c >> 1 & 1) * 2 + (d >> 1 & 1)
                    column = (c & 1) * 2 + (d & 1)
                    pairs[pl.ds(block * rows + tile, 8), pl.ds(column * depth, depth)] = value
            return carry

        lax.fori_loop(0, tiles, body, 0)
        section = split_dot(pairs[...], table_z[...], False)
        for group in range(4):
            part = section[group * 4 * rows : (group + 1) * 4 * rows]
            terms[half, group] = split_dot(table_y[...], part, True)

    def term(a, other, half):
        return terms[half, a * 2 + other]

    mine, off = parity, 1 - parity
    sent = []

    def outgoing(source, landing, dx):
        group = []
        for dy in range(ny):
            if (dx, dy) == (0, 0):
                continue
            index = len(sent)
            copy = pltpu.make_async_remote_copy(
                src_ref=source,
                dst_ref=landing.at[dy],
                send_sem=term_send.at[index],
                recv_sem=term_recv.at[index],
                device_id=peer(dx, dy),
                device_id_type=MESH,
            )
            group.append(copy)
            sent.append(copy)
        return group

    low_copies = outgoing(to_low, from_high, -1)
    high_copies = outgoing(to_high, from_low, 1)
    own_copies = outgoing(to_own, from_own, 0)

    for upper in (1 - parity, parity):
        @pl.when(upper == 1)
        def _():
            receive(-1)

        @pl.when(upper == 0)
        def _():
            receive(1)

        beside(prepare, 0, top, upper)
        beside(join, 0, top - 1, upper)
        beside(gather, 1, top - 1, upper)
        beside(first_step, 1, top - 1, upper)
        beside(second_step, 2, top - 2, upper)
        beside(operator, 3, top - 3, upper)
        products(upper)

        @pl.when(upper == 1)
        def _():
            to_high[...] = term(off, off, 1) + pltpu.roll(term(off, mine, 1), 64, 1)
            for copy in high_copies:
                copy.start()

        @pl.when(upper == 0)
        def _():
            to_low[...] = term(off, off, 0) + pltpu.roll(term(off, mine, 0), 64, 1)
            for copy in low_copies:
                copy.start()

    to_own[0] = term(mine, off, 0)
    to_own[1] = term(mine, mine, 0) + term(mine, mine, 1)
    to_own[2] = term(mine, off, 1)
    for copy in own_copies:
        copy.start()
    stored = pltpu.make_async_copy(phi_a.at[:, own, main, :], basis_hbm, out_sem)
    stored.start()

    for copy in sent:
        copy.wait_recv()

    before = [to_own[0], to_own[1], to_own[2]]
    for dy in range(ny):
        if dy:
            before = [before[i] + from_own[dy, i] for i in range(3)]
        before[0] = before[0] + pltpu.roll(from_low[dy], 64, 1)
        before[1] = before[1] + from_low[dy] + from_high[dy]
        before[2] = before[2] + pltpu.roll(from_high[dy], 64, 1)
    for xo in range(3):
        tile = before[xo] * COARSE_SCALE
        short = 128 - tile.shape[0]
        if short:
            tile = jnp.concatenate([tile, jnp.zeros((short, 128), jnp.float32)], axis=0)
        turned = tile.T
        for yo in range(3):
            for zo in range(3):
                coarse_ref[9 * xo + 3 * yo + zo, 0] = turned[
                    zo * count_z : (zo + 1) * count_z, yo * count_y : (yo + 1) * count_y
                ]

    for copy in copies.values():
        copy.wait_send()
    for copy in sent:
        copy.wait_send()
    stored.wait()


def shards(classes, support_mask):
    nx, ny = lax.axis_size("gx"), lax.axis_size("gy")
    width, rows, depth = classes.shape
    wide, deep = rows + EDGE, width + 2 * HALO
    count_y, count_z = rows * ny // 8, depth // 8
    lines = 3 * count_y
    partners = 3 * ny - 1
    halos = 4 * HALO + (3 if ny == 2 else 6)
    plane = lambda *lead: pltpu.VMEM((*lead, wide, depth), jnp.float32)
    return pl.pallas_call(
        functools.partial(kernel, nx, ny),
        out_shape=(
            jax.ShapeDtypeStruct((8, width, rows, depth), jnp.float32),
            jax.ShapeDtypeStruct((27, 1, count_z, count_y), jnp.float32),
        ),
        in_specs=[pl.BlockSpec(memory_space=pl.ANY)],
        out_specs=(
            pl.BlockSpec(memory_space=pl.ANY),
            pl.BlockSpec(memory_space=pltpu.VMEM),
        ),
        scratch_shapes=[
            pltpu.VMEM((2, deep, wide, depth), jnp.int32),
            pltpu.VMEM((2, width, EDGE, depth), jnp.int32),
            pltpu.VMEM((2, 2, deep, EDGE, depth) if ny > 2 else (1, 1, 1, EDGE, depth), jnp.int32),
            plane(deep),
            plane(deep),
            plane(deep),
            plane(deep),
            plane(deep),
            plane(4),
            plane(8, deep),
            plane(8, deep),
            pltpu.VMEM((8, width, rows, depth), jnp.float32),
            pltpu.VMEM((16 * rows, 4 * depth), jnp.float32),
            pltpu.VMEM((lines, 4 * rows), jnp.bfloat16),
            pltpu.VMEM((4 * depth, 128), jnp.bfloat16),
            pltpu.VMEM((2, 4, lines, 128), jnp.float32),
            pltpu.VMEM((lines, 128), jnp.float32),
            pltpu.VMEM((lines, 128), jnp.float32),
            pltpu.VMEM((3, lines, 128), jnp.float32),
            pltpu.VMEM((ny, lines, 128), jnp.float32),
            pltpu.VMEM((ny, lines, 128), jnp.float32),
            pltpu.VMEM((ny, 3, lines, 128), jnp.float32),
            pltpu.SemaphoreType.DMA((2,)),
            pltpu.SemaphoreType.DMA((halos,)),
            pltpu.SemaphoreType.DMA((halos,)),
            pltpu.SemaphoreType.DMA((partners,)),
            pltpu.SemaphoreType.DMA((partners,)),
            pltpu.SemaphoreType.DMA,
        ],
        compiler_params=pltpu.CompilerParams(
            collective_id=0, has_side_effects=True, vmem_limit_bytes=32 * 1024 * 1024
        ),
    )(jnp.stack([classes, support_mask]))


def solution(mesh):
    in_specs = (P("gx", "gy", None), P("gx", "gy", None))
    out_specs = (P(None, "gx", "gy", None), P(None, "gx", None, None))
    return jax.shard_map(shards, mesh=mesh, in_specs=in_specs, out_specs=out_specs, check_vma=False)
```
